32 devices in a mesh: inline: 4 (over y, x), xline: 8 (over z, core).
Axes of the slice: x: 2, y: 2, z: 4, core: 2. Of those that a mesh axis runs over, the one named last changes fastest.
Arguments:
- base_volume: float32 [64, 128, 256], P('inline', 'xline'), may hold values from -6 to 6
- vintage_traces: float32 [32768, 256], P(('inline', 'xline')), may hold values from -6 to 6
- dest_device: int32 [32768, 1], P(('inline', 'xline')), may hold values from 0 to 31; in each aligned block of 1024 rows (0 to 1023, 1024 to 2047, ...) at most 64 rows name the same one
- dest_slot: int32 [32768], P(('inline', 'xline')), may hold values from 0 to 255
- vintage_id: int32 [32768], P(('inline', 'xline')), may hold values from 0 to 3
- vintage_gains: float32 [4], replicated, may hold values from 0.5 to 2
- dictionary: bfloat16 [512, 512], replicated, may hold values from -0.09375 to 0.09375
Outputs:
- codes: float32 [16, 32, 64, 512], P('inline', 'xline')
- residual: float32 [64, 128, 256], P('inline', 'xline')
The draws below stay inside these ranges and needn't reach their ends.
Inputs may be any that keep to these rules, and one draw needn't show every extreme that they name: `dest_device`: among the traces of one device, no tile is named more than 64 times, a bound that some block reaches.
All inputs are finite; a program needn't handle non-finite values.
Results may differ from the reference program's by a relative error of at most 0.0022.
Values may be sent and summed in bfloat16 or wider, within the bound.
A program may use at most 64 MiB of HBM per device.

```python
import math
import jax
import jax.numpy as jnp
import numpy as np
from jax import lax

SIDE = 16
NT = 256
ATOMS = 512
PATCH = 8
VT = 1024
NV = 4
CAP = 64
TRACES = 32768
ROWS = 64
COLS = 128
N_INLINE = 4
N_XLINE = 8
DEVICES = 32


def place_ends(array, stream_key, low, largest):
    longest = array.shape.index(max(array.shape))
    spots = []
    for shift in (0, 1):
        where = [jax.random.randint(jax.random.fold_in(stream_key, axis), (), 0, length) for axis, length in enumerate(array.shape)]
        where[longest] = (where[longest] + shift) % array.shape[longest]
        spots.append(tuple(where))
    return array.at[spots[0]].set(low).at[spots[1]].set(largest)


def levels(stream_key, dims, pieces, smallest, largest):
    level = 1.0
    for dim, shards_of in pieces:
        draws = jax.random.uniform(jax.random.fold_in(jax.random.fold_in(stream_key, 6), dim), (shards_of,), jnp.float32, smallest / len(pieces), largest / len(pieces))
        level = level * jnp.repeat(jnp.exp(draws), dims[dim] // shards_of).reshape((-1,) + (1,) * (len(dims) - 1 - dim))
    return level


def assign_block(key, own, number, rows, number_of, top, most, slope):
    order = jax.random.permutation(key, number_of)
    crowded, usual = shares(number_of, rows * top, most, slope, True), shares(number_of, rows * top, most, slope, False)
    places = jnp.arange(number_of)

    def named(lengths, turn):
        used = int((lengths > 0).sum())
        fixed = max(1, used // 4)
        moved = fixed + (places - fixed + turn * (used - fixed)) % max(1, number_of - fixed)
        return jnp.zeros((number_of,), jnp.int32).at[order[jnp.where(places < fixed, places, moved)]].set(jnp.asarray(lengths, jnp.int32))

    lengths = jnp.where(number % 4 == 0, named(crowded, number // 4), named(usual, number - number // 4 - 1))
    mixed = jax.random.permutation(jax.random.fold_in(own, 3), number_of)
    giver, receiver = mixed[0:number_of // 2 * 2:2], mixed[1:number_of // 2 * 2:2]
    margin = jnp.minimum(lengths[giver] - 1, most - lengths[receiver]) // 2
    margin = jnp.where((giver == order[0]) | (receiver == order[0]) | (lengths[receiver] == 0), 0, jnp.maximum(margin, 0))
    moved = jax.random.randint(jax.random.fold_in(own, 4), (number_of // 2,), 0, 1 << 20) % (margin + 1)
    lengths = lengths.at[giver].add(-moved).at[receiver].add(moved)
    members = jnp.searchsorted(jnp.cumsum(lengths), jnp.arange(rows * top), side="right").astype(jnp.int32)
    grid = members.reshape(top, rows).T
    grid = grid[jax.random.permutation(jax.random.fold_in(own, 1), rows)]
    turn = jax.random.randint(jax.random.fold_in(own, 2), (rows, 1), 0, top)
    return jnp.take_along_axis(grid, (jnp.arange(top)[None, :] + turn) % top, axis=1)


def shares(amount, total, bound, slope, full):
    weights = [(1 << 20) // math.isqrt(grade ** slope) + 1 for grade in range(1, amount + 1)]
    largest = bound if full else min(bound, max(-(-total // amount), total * weights[0] // sum(weights)))
    least = 1 if total - largest >= amount - 1 else 0
    counts, rest = [largest] + [least] * (amount - 1), total - largest - least * (amount - 1)
    while rest > 0:
        candidates = [i for i in range(1, amount) if counts[i] < largest] or [i for i in range(1, amount) if counts[i] < bound]
        whole, budget = sum([weights[i] for i in candidates]), rest
        for i in candidates:
            addition = min(bound - counts[i], max(1, budget * weights[i] // whole), rest)
            counts[i] = counts[i] + addition
            rest = rest - addition
    return np.array(counts)


def scatter_about(rng, shape, width, reach, split=(), kind=jnp.bfloat16):
    gain = levels(rng, shape, split, -0.22, 0.18) if split else 1.0
    values = jax.random.normal(rng, shape, jnp.float32) * width * gain
    return jnp.minimum(jnp.maximum(values, -reach), reach).astype(kind)


def setup_inputs(seed: int = 0) -> dict:
    splits = jax.random.split(jax.random.key(seed), 8)
    base_volume = scatter_about(splits[0], (ROWS, COLS, NT), 1.0, 6.0, ((0, 4), (1, 8)), jnp.float32)
    vintage_traces = scatter_about(splits[1], (TRACES, NT), 1.0, 6.0, ((0, 32),), jnp.float32)
    dest_device_keys = jax.random.split(jax.random.fold_in(splits[2], 1), TRACES // VT)
    dest_device_turns = jax.random.permutation(jax.random.fold_in(splits[2], 3), TRACES // VT)
    dest_device = jax.vmap(lambda own, number: assign_block(jax.random.fold_in(splits[2], 2), own, number, VT, DEVICES, 1, CAP, 2))(dest_device_keys, dest_device_turns).reshape((TRACES, 1))
    dest_slot = place_ends(jax.random.randint(splits[3], (TRACES,), 0, SIDE * SIDE), jax.random.fold_in(splits[3], 1), 0, (SIDE * SIDE) - 1).astype(jnp.int32)
    vintage_id = place_ends(jax.random.randint(splits[4], (TRACES,), 0, NV), jax.random.fold_in(splits[4], 1), 0, NV - 1).astype(jnp.int32)
    vintage_gains = jnp.clip(jnp.exp(jax.random.uniform(splits[5], (NV,), jnp.float32, math.log(0.5), math.log(2.0))), 0.5, 2.0)
    dictionary = scatter_about(splits[6], (PATCH * PATCH * PATCH, ATOMS), 4096 ** -0.5, 0.09375)
    return dict(base_volume=base_volume, vintage_traces=vintage_traces, dest_device=dest_device, dest_slot=dest_slot, vintage_id=vintage_id, vintage_gains=vintage_gains, dictionary=dictionary)


step_size = 0.25
threshold = 0.02


def shrink_codes(values):
    return values - jnp.clip(values, -threshold, threshold)


def correlate(field_half, dict_blocks):
    row_count, col_count, time_count = field_half.shape
    patch_i, patch_j, patch_k = row_count // 4, col_count // 4, time_count // 4
    padded = jnp.pad(field_half.astype(jnp.float32), ((0, 4), (0, 4), (0, 4)))
    padded = padded.reshape(patch_i + 1, 4, patch_j + 1, 4, patch_k + 1, 4)
    atom_count = dict_blocks.shape[-1]

    def one_row(row_index):
        row_slab = lax.dynamic_slice_in_dim(padded, row_index, 2, 0)
        running = jnp.zeros((patch_j, patch_k, atom_count), jnp.float32)
        for shift_a in (0, 1):
            for shift_b in (0, 1):
                for shift_c in (0, 1):
                    block_piece = row_slab[shift_a][:, shift_b:shift_b + patch_j, :, shift_c:shift_c + patch_k, :]
                    running = running + jnp.einsum('ajbkc,abcn->jkn', block_piece, dict_blocks[shift_a, :, shift_b, :, shift_c, :, :])
        return running

    return lax.map(one_row, jnp.arange(patch_i, dtype=jnp.int32))


def place_part(contrib, shift_a, patch_j, patch_k):
    output = jnp.zeros((4, patch_j, 4, patch_k, 4), jnp.float32)
    for shift_b in (0, 1):
        for shift_c in (0, 1):
            block_piece = contrib[:, :, shift_a, :, shift_b, :, shift_c, :].transpose(2, 0, 3, 1, 4)
            moved = jnp.pad(block_piece, ((0, 0), (shift_b, 0), (0, 0), (shift_c, 0), (0, 0)))
            output = output + moved[:, :patch_j, :, :patch_k, :]
    return output


def reconstruct(codes_half, dict_float):
    patch_i, patch_j, patch_k, atom_count = codes_half.shape

    def advance(carried, code_row):
        contrib = jnp.einsum('jkn,en->jke', code_row.astype(jnp.float32), dict_float)
        contrib = contrib.reshape(patch_j, patch_k, 2, 4, 2, 4, 2, 4)
        current = place_part(contrib, 0, patch_j, patch_k) + carried
        return place_part(contrib, 1, patch_j, patch_k), current

    start = jnp.zeros((4, patch_j, 4, patch_k, 4), jnp.float32)
    unused, rows_out = lax.scan(advance, start, codes_half)
    return rows_out.reshape(patch_i * 4, patch_j * 4, patch_k * 4)


def reference(base_volume, vintage_traces, dest_device, dest_slot, vintage_id, vintage_gains, dictionary):
    tile_side = base_volume.shape[0] // N_INLINE
    weighted = vintage_gains[vintage_id][:, None] * vintage_traces
    target = dest_device[:, 0]
    row_at = (target // N_XLINE) * tile_side + dest_slot // tile_side
    col_at = (target % N_XLINE) * tile_side + dest_slot % tile_side
    stack = jnp.zeros(base_volume.shape, jnp.float32).at[row_at, col_at].add(weighted)
    fold = jnp.zeros(base_volume.shape[:2], jnp.float32).at[row_at, col_at].add(jnp.float32(1.0))
    merged = (base_volume + stack) / (1.0 + fold)[:, :, None]
    dict_float = dictionary.astype(jnp.float32)
    dict_blocks = dict_float.reshape(2, 4, 2, 4, 2, 4, dict_float.shape[1])
    first = shrink_codes(step_size * correlate(merged.astype(jnp.bfloat16), dict_blocks))
    recon = reconstruct(first.astype(jnp.bfloat16), dict_float)
    residual = merged - recon
    codes = shrink_codes(first + step_size * correlate(residual.astype(jnp.bfloat16), dict_blocks))
    return codes, residual
```

```python
import functools
import jax
import jax.numpy as jnp
from jax import lax
from jax.experimental import pallas as pl
from jax.experimental.pallas import tpu as pltpu
from jax.sharding import PartitionSpec as P

step_size = 0.25
threshold = 0.02
WIRE = jnp.int16
FULL = 32768.0
MESH = pl.DeviceIdType.MESH
F32, BF16 = jnp.float32, jnp.bfloat16


def shrink_codes(values):
    return values - jnp.clip(values, -threshold, threshold)


def iota(shape, dim):
    return lax.broadcasted_iota(jnp.int32, shape, dim)


def split_half(x):
    hi = x.astype(BF16)
    return hi, (x - hi.astype(F32)).astype(BF16)


def exchange_kernel(nx, n, cap, w_ref, tgt_ref, slot_ref, unit_ref, base_ref, out_ref, whl, rank, grid_sel,
                    meta_out, meta_in, send, got, acc, fold, basep, moves,
                    send_sem, recv_sem, msend_sem, mrecv_sem):
    me = lax.axis_index("inline") * nx + lax.axis_index("xline")
    side, time_len = base_ref.shape[0], base_ref.shape[2]
    blocks = side // 4
    bins = side * side
    traces = w_ref.shape[0]
    q = 256 // cap
    chunks = n // q

    def where_is(p):
        return (p // nx, p % nx)

    barrier = pltpu.get_barrier_semaphore()

    @pl.loop(1, n)
    def _(off):
        pl.semaphore_signal(barrier, inc=1, device_id=where_is((me + off) % n), device_id_type=MESH)

    hi, lo = split_half(w_ref[...])
    whl[:, :time_len] = hi
    whl[:, time_len:] = lo
    tri = (iota((128, 128), 0) <= iota((128, 128), 1)).astype(F32).astype(BF16)
    base_count = jnp.zeros((n, 1), F32)
    for b in range(traces // 128):
        mine = tgt_ref[:, b * 128:(b + 1) * 128] == iota((n, 128), 0)
        one = jnp.where(mine, 1.0, 0.0)
        cum = jnp.dot(one.astype(BF16), tri, preferred_element_type=F32) + base_count
        rank[:, b * 128:(b + 1) * 128] = jnp.where(mine, cum - 1.0, -1.0)
        base_count = base_count + jnp.sum(one, axis=1, keepdims=True)
    slot = slot_ref[...]
    r, c = slot // side, slot % side
    binned = ((r // 4) * blocks + c // 4) * 16 + (r % 4) * 4 + c % 4
    first_row = iota((16, traces), 0) == 0
    about = jnp.where(first_row, (binned + 1).astype(F32), unit_ref[...]).astype(BF16)
    my_q = me % q
    lane_from, lane_to = iota((256, 256), 0), iota((256, 256), 1)
    for i in range(q):
        move = (lane_from - my_q * cap == lane_to - i * cap) & (lane_to // cap == i)
        moves[i] = jnp.where(move, 1.0, 0.0).astype(BF16)
    for bi in range(blocks):
        for bj in range(blocks):
            for a in range(4):
                at = (bi * blocks + bj) * 16 + a * 4
                basep[at:at + 4, :] = base_ref[4 * bi + a, 4 * bj:4 * bj + 4, :]
    acc[...] = jnp.zeros_like(acc)
    fold[...] = jnp.zeros_like(fold)

    @pl.loop(0, chunks)
    def _(step):
        ch = (me // q + 1 + step) % chunks
        want = iota((cap, traces), 0).astype(F32)
        for i in range(q):
            row = rank[pl.ds(ch * q + i, 1), :]
            grid_sel[i * cap:(i + 1) * cap, :] = jnp.where(row == want, 1.0, 0.0).astype(BF16)
        sel = grid_sel[...]
        picked = jnp.dot(sel, whl[...], preferred_element_type=F32)
        packed = (picked[:, :time_len] + picked[:, time_len:]).astype(jnp.int32).astype(WIRE)
        names = lax.dot_general(about, sel, (((1,), (1,)), ((), ())), preferred_element_type=F32)
        meta_out[ch] = names[0:2, :]
        for i in range(q):
            send[ch * q + i] = packed[i * cap:(i + 1) * cap, :]

        @pl.when(step == 0)
        def _():
            pl.semaphore_wait(barrier, n - 1)

        for i in range(q):
            p = ch * q + i

            @pl.when(p != me)
            def _():
                pltpu.make_async_remote_copy(
                    meta_out.at[ch], meta_in.at[me], msend_sem, mrecv_sem.at[me],
                    device_id=where_is(p), device_id_type=MESH).start()
                pltpu.make_async_remote_copy(
                    send.at[p], got.at[me], send_sem, recv_sem.at[me],
                    device_id=where_is(p), device_id_type=MESH).start()

            @pl.when(p == me)
            def _():
                meta_in[me] = meta_out[ch]
                got[me] = send[p]

    @pl.loop(0, chunks)
    def _(step):
        ch = (me // q + chunks - 1 - step + chunks) % chunks
        names = jnp.zeros((16, 256), F32)
        for i in range(q):
            src = ch * q + i

            @pl.when(src != me)
            def _():
                pltpu.make_async_remote_copy(
                    meta_out.at[0], meta_in.at[src], msend_sem, mrecv_sem.at[src],
                    device_id=where_is(src), device_id_type=MESH).wait_recv()
                pltpu.make_async_remote_copy(
                    send.at[src], got.at[src], send_sem, recv_sem.at[src],
                    device_id=where_is(src), device_id_type=MESH).wait_recv()

            both = meta_in[src]
            row = jnp.where(iota((16, 256), 0) == 0, both[0:1, :], both[1:2, :]).astype(BF16)
            names = names + jnp.dot(row, moves[i], preferred_element_type=F32)
        hit = jnp.where(names[0:1, :] == (iota((bins, 256), 0) + 1).astype(F32), 1.0, 0.0)
        rows = got[pl.ds(ch * q, q)].astype(jnp.int32).astype(F32).reshape(256, time_len)
        hi, lo = split_half(rows)
        half = (hit * names[1:2, :]).astype(BF16)
        acc[...] += jnp.dot(half, hi, preferred_element_type=F32) + jnp.dot(half, lo, preferred_element_type=F32)
        fold[...] += hit

    count = jnp.sum(fold[...], axis=1, keepdims=True)
    out_ref[...] = (basep[...] + acc[...] * (1.0 / FULL)) / (1.0 + count)
    all_data = send.at[pl.ds(0, n - 1)]
    pltpu.make_async_copy(all_data, got.at[pl.ds(0, n - 1)], send_sem).wait()
    pltpu.make_async_copy(meta_in.at[pl.ds(0, n - 1)], meta_in.at[pl.ds(0, n - 1)], msend_sem).wait()


def patches_of(v_ref, i, blocks):
    rows = []
    for j in range(blocks):
        rows.append(jnp.concatenate(
            [v_ref[i + sa, j + sb] for sa in (0, 1) for sb in (0, 1)], axis=1))
    return jnp.concatenate(rows, axis=0)


def fold_time(x):
    rolled = pltpu.roll(x, 64, 1)
    rolled = pltpu.roll(rolled, 1, 0)
    return x + jnp.where(iota(x.shape, 0) == 0, 0.0, rolled)


def widen_time(x):
    ahead = pltpu.roll(pltpu.roll(x, 64, 1), x.shape[0] - 1, 0)
    ahead = jnp.where(iota(x.shape, 0) == x.shape[0] - 1, 0.0, ahead)
    return jnp.where(iota(x.shape, 1) < 64, x, ahead)


def ista_kernel(ni, nx, m_ref, d_ref, v1_ref, v2_ref, res_ref, tsc, cube, spread, out_half,
                from_row, from_col, from_cor, ssem, rsem):
    mi, mx = lax.axis_index("inline"), lax.axis_index("xline")
    blocks = v1_ref.shape[0] - 1
    kt = v1_ref.shape[2]
    cells, time_len = m_ref.shape
    barrier = pltpu.get_barrier_semaphore()

    def greet(di, dx):
        ok = (mi + di >= 0) & (mi + di < ni) & (mx + dx >= 0) & (mx + dx < nx)

        @pl.when(ok)
        def _():
            pl.semaphore_signal(barrier, inc=1, device_id=(mi + di, mx + dx), device_id_type=MESH)

    around = [(-1, 0), (0, -1), (-1, -1), (1, 0), (0, 1), (1, 1)]
    for di, dx in around:
        greet(di, dx)

    has_prev = [mi > 0, mx > 0, (mi > 0) & (mx > 0)]
    has_next = [mi < ni - 1, mx < nx - 1, (mi < ni - 1) & (mx < nx - 1)]
    steps = [(1, 0), (0, 1), (1, 1)]

    def halo_copies(v_ref, slot):
        pairs = [(v_ref.at[0, pl.ds(0, blocks)], v_ref.at[blocks, pl.ds(0, blocks)]),
                 (v_ref.at[pl.ds(0, blocks), 0], v_ref.at[pl.ds(0, blocks), blocks]),
                 (v_ref.at[0, 0], v_ref.at[blocks, blocks])]
        return [pltpu.make_async_remote_copy(
            src, dst, ssem.at[slot, m], rsem.at[slot, m],
            device_id=(mi - steps[m][0], mx - steps[m][1]), device_id_type=MESH)
            for m, (src, dst) in enumerate(pairs)]

    def clear_edges(v_ref):
        blank = jnp.zeros((kt, 128), BF16)

        @pl.when(mi == ni - 1)
        def _():
            for j in range(blocks + 1):
                v_ref[blocks, j] = blank

        @pl.when(mx == nx - 1)
        def _():
            for i in range(blocks + 1):
                v_ref[i, blocks] = blank

    def run(copies, guards, what):
        for copy, guard in zip(copies, guards):
            @pl.when(guard)
            def _():
                getattr(copy, what)()

    lane = iota((kt, 128), 1) // 16
    turned = m_ref[...].T
    for col in range(cells // 128):
        tsc[col, time_len:, :] = jnp.zeros((8, 128), F32)
        tsc[col, :time_len, :] = turned[:, col * 128:(col + 1) * 128]
    clear_edges(v1_ref)
    clear_edges(v2_ref)
    for col in range(cells // 128):
        parts = [tsc[col, pl.ds(g, kt, stride=4), :] for g in range(8)]
        for e in range(8):
            b = col * 8 + e
            v = parts[e]
            for g in range(8):
                if g != e:
                    v = jnp.where(lane == g, pltpu.roll(parts[g], ((g - e) * 16) % 128, 1), v)
            cube[b] = v
            v1_ref[b // blocks, b % blocks] = v.astype(BF16)
    up, down = (mi > 0).astype(jnp.int32), (mi < ni - 1).astype(jnp.int32)
    west, east = (mx > 0).astype(jnp.int32), (mx < nx - 1).astype(jnp.int32)
    pl.semaphore_wait(barrier, up + down + west + east + up * west + down * east)
    sends = halo_copies(v1_ref, 0)
    run(sends, has_prev, "start")
    run(sends, has_next, "wait_recv")

    for i in range(blocks + 1):
        for j in range(blocks + 1):
            spread[i, j] = jnp.zeros((kt, 128), F32)
    for i in range(blocks):
        first = shrink_codes(step_size * jnp.dot(patches_of(v1_ref, i, blocks), d_ref[...],
                                                 preferred_element_type=F32))
        back = lax.dot_general(first.astype(BF16), d_ref[...], (((1,), (1,)), ((), ())),
                               preferred_element_type=F32)
        for j in range(blocks):
            for sa in (0, 1):
                for sb in (0, 1):
                    g = (2 * sa + sb) * 128
                    spread[i + sa, j + sb] += back[j * kt:(j + 1) * kt, g:g + 128]
    for j in range(blocks):
        out_half[j] = fold_time(spread[blocks, j]).astype(BF16)
        out_half[blocks + j] = fold_time(spread[j, blocks]).astype(BF16)
    out_half[2 * blocks] = fold_time(spread[blocks, blocks]).astype(BF16)
    ends = [(out_half.at[pl.ds(0, blocks)], from_row), (out_half.at[pl.ds(blocks, blocks)], from_col),
            (out_half.at[2 * blocks], from_cor)]
    terms = [pltpu.make_async_remote_copy(
        src, dst, ssem.at[1, m], rsem.at[1, m],
        device_id=(mi + steps[m][0], mx + steps[m][1]), device_id_type=MESH)
        for m, (src, dst) in enumerate(ends)]
    run(terms, has_next, "start")

    for guard, ref in zip(has_prev, (from_row, from_col, from_cor)):
        @pl.when(jnp.logical_not(guard))
        def _():
            ref[...] = jnp.zeros_like(ref)

    def finish(i, j, more):
        b = i * blocks + j
        whole = fold_time(spread[i, j])
        for term in more:
            whole = whole + term.astype(F32)
        left = cube[b] - whole
        cube[b] = left
        v2_ref[i, j] = widen_time(left).astype(BF16)

    for i in range(1, blocks):
        for j in range(1, blocks):
            finish(i, j, [])
    run(terms, has_prev, "wait_recv")
    finish(0, 0, [from_row[0], from_col[0], from_cor[...]])
    for j in range(1, blocks):
        finish(0, j, [from_row[j]])
        finish(j, 0, [from_col[j]])
    last = halo_copies(v2_ref, 2)
    run(last, has_prev, "start")

    for col in range(cells // 128):
        parts = [cube[col * 8 + e] for e in range(8)]
        for s in range(4):
            v = parts[s]
            for e in range(8):
                if e != s:
                    v = jnp.where(lane == e, pltpu.roll(parts[e], ((e - s) * 16) % 128, 1), v)
            tsc[col, pl.ds(s, kt, stride=4), :] = v
    flat = jnp.concatenate([tsc[col, :time_len, :] for col in range(cells // 128)], axis=1).T
    for bi in range(blocks):
        for bj in range(blocks):
            for a in range(4):
                at = (bi * blocks + bj) * 16 + a * 4
                res_ref[4 * bi + a, 4 * bj:4 * bj + 4, :] = flat[at:at + 4, :]
    run(last, has_next, "wait_recv")
    run(sends, has_prev, "wait_send")
    run(terms, has_next, "wait_send")
    run(last, has_prev, "wait_send")


def codes_kernel(v1_ref, v2_ref, d_ref, out_ref):
    blocks = v1_ref.shape[0] - 1
    i = pl.program_id(0)
    first = shrink_codes(step_size * jnp.dot(patches_of(v1_ref, i, blocks), d_ref[...],
                                             preferred_element_type=F32))
    again = step_size * jnp.dot(patches_of(v2_ref, i, blocks), d_ref[...], preferred_element_type=F32)
    out_ref[...] = shrink_codes(first + again).reshape(out_ref.shape)


def body(ni, nx, base_volume, vintage_traces, dest_device, dest_slot, vintage_id, vintage_gains, dictionary):
    side, time_len = base_volume.shape[0], base_volume.shape[2]
    n = ni * nx
    traces = vintage_traces.shape[0]
    cap = 2 * traces // n
    blocks, kt, cells = side // 4, time_len // 4, side * side
    atoms = dictionary.shape[1]
    table = vintage_id[:, None] == jnp.arange(vintage_gains.shape[0], dtype=jnp.int32)[None, :]
    gain = jnp.sum(jnp.where(table, vintage_gains[None, :], 0.0), axis=1)
    weighted = vintage_traces * gain[:, None]
    largest = jnp.max(jnp.abs(weighted), axis=1)
    unit = jnp.full((traces,), 16.0, F32)
    for power in range(3, -31, -1):
        unit = jnp.where(largest < 2.0 ** power, 2.0 ** power, unit)
    whole_steps = jnp.clip(jnp.round(weighted * (FULL / unit)[:, None]), 1.0 - FULL, FULL - 1.0)
    ordered = dictionary.reshape(2, 4, 2, 4, 8, atoms).transpose(0, 2, 4, 1, 3, 5).reshape(512, atoms)
    vmem = pl.BlockSpec(memory_space=pltpu.VMEM)
    dma = pltpu.SemaphoreType.DMA
    merged = pl.pallas_call(
        functools.partial(exchange_kernel, nx, n, cap),
        out_shape=jax.ShapeDtypeStruct((cells, time_len), F32),
        in_specs=[vmem] * 5, out_specs=vmem,
        scratch_shapes=[
            pltpu.VMEM((traces, 2 * time_len), BF16), pltpu.VMEM((n, traces), F32),
            pltpu.VMEM((256, traces), BF16), pltpu.VMEM((n * cap // 256, 2, 256), F32),
            pltpu.VMEM((n, 2, 256), F32), pltpu.VMEM((n, cap, time_len), WIRE),
            pltpu.VMEM((n, cap, time_len), WIRE), pltpu.VMEM((cells, time_len), F32),
            pltpu.VMEM((cells, 256), F32), pltpu.VMEM((cells, time_len), F32),
            pltpu.VMEM((256 // cap, 256, 256), BF16),
            dma, dma((n,)), dma, dma((n,))],
        compiler_params=pltpu.CompilerParams(collective_id=0, has_side_effects=True,
                                             vmem_limit_bytes=40 << 20),
        name="exchange",
    )(whole_steps, dest_device.reshape(1, traces), dest_slot.reshape(1, traces), unit.reshape(1, traces), base_volume)
    halo = (blocks + 1, blocks + 1, kt, 128)
    v1, v2, residual = pl.pallas_call(
        functools.partial(ista_kernel, ni, nx),
        out_shape=(jax.ShapeDtypeStruct(halo, BF16), jax.ShapeDtypeStruct(halo, BF16),
                   jax.ShapeDtypeStruct(base_volume.shape, F32)),
        in_specs=[vmem] * 2, out_specs=(vmem,) * 3,
        scratch_shapes=[
            pltpu.VMEM((cells // 128, time_len + 8, 128), F32), pltpu.VMEM((blocks * blocks, kt, 128), F32),
            pltpu.VMEM(halo, F32), pltpu.VMEM((2 * blocks + 1, kt, 128), BF16),
            pltpu.VMEM((blocks, kt, 128), BF16), pltpu.VMEM((blocks, kt, 128), BF16),
            pltpu.VMEM((kt, 128), BF16), dma((3, 3)), dma((3, 3))],
        compiler_params=pltpu.CompilerParams(collective_id=1, has_side_effects=True,
                                             vmem_limit_bytes=40 << 20),
        name="ista",
    )(merged, ordered)
    whole = lambda *shape: pl.BlockSpec(shape, lambda i: (0,) * len(shape))
    codes = pl.pallas_call(
        codes_kernel,
        grid=(blocks,),
        out_shape=jax.ShapeDtypeStruct((blocks, blocks, kt, atoms), F32),
        in_specs=[whole(*halo), whole(*halo), whole(512, atoms)],
        out_specs=pl.BlockSpec((1, blocks, kt, atoms), lambda i: (i, 0, 0, 0)),
        compiler_params=pltpu.CompilerParams(vmem_limit_bytes=40 << 20),
        name="codes",
    )(v1, v2, ordered)
    return codes, residual


def solution(mesh):
    in_specs = (
        P("inline", "xline", None),
        P(("inline", "xline"), None),
        P(("inline", "xline"), None),
        P(("inline", "xline")),
        P(("inline", "xline")),
        P(),
        P(),
    )
    out_specs = (P("inline", "xline", None, None), P("inline", "xline", None))
    return jax.shard_map(functools.partial(body, mesh.shape["inline"], mesh.shape["xline"]),
                         mesh=mesh, in_specs=in_specs, out_specs=out_specs, check_vma=False)
```

```python
import functools
import jax
import jax.numpy as jnp
from jax import lax
from jax.experimental import pallas as pl
from jax.experimental.pallas import tpu as pltpu
from jax.sharding import PartitionSpec as P

step_size = 0.25
threshold = 0.02
WIRE = jnp.int16
FULL = 32768.0
MESH = pl.DeviceIdType.MESH
F32, BF16 = jnp.float32, jnp.bfloat16


def shrink_codes(values):
    return values - jnp.clip(values, -threshold, threshold)


def iota(shape, dim):
    return lax.broadcasted_iota(jnp.int32, shape, dim)


def split_half(x):
    hi = x.astype(BF16)
    return hi, (x - hi.astype(F32)).astype(BF16)


def exchange(while_waiting, nx, n, cap, w_ref, tgt_ref, slot_ref, unit_ref, base_ref, d_in, out_ref, d_ref, whl, rank, grid_sel,
                    meta_out, meta_in, send, got, acc, fold, basep, moves,
                    send_sem, recv_sem, msend_sem, mrecv_sem):
    me = lax.axis_index("inline") * nx + lax.axis_index("xline")
    side, time_len = base_ref.shape[0], base_ref.shape[2]
    blocks = side // 4
    bins = side * side
    traces = w_ref.shape[0]
    q = 256 // cap
    chunks = n // q

    def where_is(p):
        return (p // nx, p % nx)

    barrier = pltpu.get_barrier_semaphore()

    @pl.loop(1, n)
    def _(off):
        pl.semaphore_signal(barrier, inc=1, device_id=where_is((me + off) % n), device_id_type=MESH)

    hi, lo = split_half(w_ref[...])
    whl[:, :time_len] = hi
    whl[:, time_len:] = lo
    tri = (iota((128, 128), 0) <= iota((128, 128), 1)).astype(F32).astype(BF16)
    base_count = jnp.zeros((n, 1), F32)
    for b in range(traces // 128):
        mine = tgt_ref[:, b * 128:(b + 1) * 128] == iota((n, 128), 0)
        one = jnp.where(mine, 1.0, 0.0)
        cum = jnp.dot(one.astype(BF16), tri, preferred_element_type=F32) + base_count
        rank[:, b * 128:(b + 1) * 128] = jnp.where(mine, cum - 1.0, -1.0)
        base_count = base_count + jnp.sum(one, axis=1, keepdims=True)
    slot = slot_ref[...]
    r, c = slot // side, slot % side
    binned = ((r // 4) * blocks + c // 4) * 16 + (r % 4) * 4 + c % 4
    first_row = iota((16, traces), 0) == 0
    about = jnp.where(first_row, (binned + 1).astype(F32), unit_ref[...]).astype(BF16)
    my_q = me % q
    lane_from, lane_to = iota((256, 256), 0), iota((256, 256), 1)
    for i in range(q):
        move = (lane_from - my_q * cap == lane_to - i * cap) & (lane_to // cap == i)
        moves[i] = jnp.where(move, 1.0, 0.0).astype(BF16)
    for bi in range(blocks):
        for bj in range(blocks):
            for a in range(4):
                at = (bi * blocks + bj) * 16 + a * 4
                basep[at:at + 4, :] = base_ref[4 * bi + a, 4 * bj:4 * bj + 4, :]
    acc[...] = jnp.zeros_like(acc)
    fold[...] = jnp.zeros_like(fold)

    @pl.loop(0, chunks)
    def _(step):
        ch = (me // q + 1 + step) % chunks
        want = iota((cap, traces), 0).astype(F32)
        for i in range(q):
            row = rank[pl.ds(ch * q + i, 1), :]
            grid_sel[i * cap:(i + 1) * cap, :] = jnp.where(row == want, 1.0, 0.0).astype(BF16)
        sel = grid_sel[...]
        picked = jnp.dot(sel, whl[...], preferred_element_type=F32)
        packed = (picked[:, :time_len] + picked[:, time_len:]).astype(jnp.int32).astype(WIRE)
        names = lax.dot_general(about, sel, (((1,), (1,)), ((), ())), preferred_element_type=F32)
        meta_out[ch] = names[0:2, :]
        for i in range(q):
            send[ch * q + i] = packed[i * cap:(i + 1) * cap, :]

        @pl.when(step == 0)
        def _():
            pl.semaphore_wait(barrier, n - 1)

        for i in range(q):
            p = ch * q + i

            @pl.when(p != me)
            def _():
                pltpu.make_async_remote_copy(
                    meta_out.at[ch], meta_in.at[me], msend_sem, mrecv_sem.at[me],
                    device_id=where_is(p), device_id_type=MESH).start()
                pltpu.make_async_remote_copy(
                    send.at[p], got.at[me], send_sem, recv_sem.at[me],
                    device_id=where_is(p), device_id_type=MESH).start()

            @pl.when(p == me)
            def _():
                meta_in[me] = meta_out[ch]
                got[me] = send[p]

    rows_of, cols_of = iota((512, 512), 0), iota((512, 512), 1)
    wanted = ((rows_of // 256) * 256 + (rows_of % 16) // 4 * 64 + (rows_of // 128 % 2) * 32
              + (rows_of % 4) * 8 + rows_of // 16 % 8)
    d_ref[...] = jnp.dot(jnp.where(wanted == cols_of, 1.0, 0.0).astype(BF16), d_in[...],
                         preferred_element_type=F32).astype(BF16)
    while_waiting()

    @pl.loop(0, chunks)
    def _(step):
        ch = (me // q + chunks - 1 - step + chunks) % chunks
        names = jnp.zeros((16, 256), F32)
        for i in range(q):
            src = ch * q + i

            @pl.when(src != me)
            def _():
                pltpu.make_async_remote_copy(
                    meta_out.at[0], meta_in.at[src], msend_sem, mrecv_sem.at[src],
                    device_id=where_is(src), device_id_type=MESH).wait_recv()
                pltpu.make_async_remote_copy(
                    send.at[src], got.at[src], send_sem, recv_sem.at[src],
                    device_id=where_is(src), device_id_type=MESH).wait_recv()

            both = meta_in[src]
            row = jnp.where(iota((16, 256), 0) == 0, both[0:1, :], both[1:2, :]).astype(BF16)
            names = names + jnp.dot(row, moves[i], preferred_element_type=F32)
        hit = jnp.where(names[0:1, :] == (iota((bins, 256), 0) + 1).astype(F32), 1.0, 0.0)
        rows = got[pl.ds(ch * q, q)].astype(jnp.int32).astype(F32).reshape(256, time_len)
        hi, lo = split_half(rows)
        half = (hit * names[1:2, :]).astype(BF16)
        acc[...] += jnp.dot(half, hi, preferred_element_type=F32) + jnp.dot(half, lo, preferred_element_type=F32)
        fold[...] += hit

    count = jnp.sum(fold[...], axis=1, keepdims=True)
    out_ref[...] = (basep[...] + acc[...] * (1.0 / FULL)) / (1.0 + count)


def exchange_end(n, send, got, meta_in, send_sem, msend_sem):
    all_data = send.at[pl.ds(0, n - 1)]
    pltpu.make_async_copy(all_data, got.at[pl.ds(0, n - 1)], send_sem).wait()
    pltpu.make_async_copy(meta_in.at[pl.ds(0, n - 1)], meta_in.at[pl.ds(0, n - 1)], msend_sem).wait()


def patches_of(v_ref, i, blocks):
    rows = []
    for j in range(blocks):
        rows.append(jnp.concatenate(
            [v_ref[i + sa, j + sb] for sa in (0, 1) for sb in (0, 1)], axis=1))
    return jnp.concatenate(rows, axis=0)


def fold_time(x):
    rolled = pltpu.roll(x, 64, 1)
    rolled = pltpu.roll(rolled, 1, 0)
    return x + jnp.where(iota(x.shape, 0) == 0, 0.0, rolled)


def widen_time(x):
    ahead = pltpu.roll(pltpu.roll(x, 64, 1), x.shape[0] - 1, 0)
    ahead = jnp.where(iota(x.shape, 0) == x.shape[0] - 1, 0.0, ahead)
    return jnp.where(iota(x.shape, 1) < 64, x, ahead)


def main_kernel(ni, nx, cap, w_ref, tgt_ref, slot_ref, unit_ref, base_ref, d_in,
                d_ref, v1_ref, v2_ref, res_ref,
                m_ref, whl, rank, grid_sel, meta_out, meta_in, send, got, acc, fold, basep, moves,
                send_sem, recv_sem, msend_sem, mrecv_sem,
                tsc, cube, spread, out_half, from_row, from_col, from_cor, ssem, rsem):
    mi, mx = lax.axis_index("inline"), lax.axis_index("xline")
    blocks = v1_ref.shape[0] - 1
    kt = v1_ref.shape[2]
    cells, time_len = m_ref.shape
    has_prev = [mi > 0, mx > 0, (mi > 0) & (mx > 0)]
    has_next = [mi < ni - 1, mx < nx - 1, (mi < ni - 1) & (mx < nx - 1)]
    steps = [(1, 0), (0, 1), (1, 1)]

    def halo_copies(v_ref, slot):
        pairs = [(v_ref.at[0, pl.ds(0, blocks)], v_ref.at[blocks, pl.ds(0, blocks)]),
                 (v_ref.at[pl.ds(0, blocks), 0], v_ref.at[pl.ds(0, blocks), blocks]),
                 (v_ref.at[0, 0], v_ref.at[blocks, blocks])]
        return [pltpu.make_async_remote_copy(
            src, dst, ssem.at[slot, m], rsem.at[slot, m],
            device_id=(mi - steps[m][0], mx - steps[m][1]), device_id_type=MESH)
            for m, (src, dst) in enumerate(pairs)]

    def clear_edges(v_ref):
        blank = jnp.zeros((kt, 128), BF16)

        @pl.when(mi == ni - 1)
        def _():
            for j in range(blocks + 1):
                v_ref[blocks, j] = blank

        @pl.when(mx == nx - 1)
        def _():
            for i in range(blocks + 1):
                v_ref[i, blocks] = blank

    def run(copies, guards, what):
        for copy, guard in zip(copies, guards):
            @pl.when(guard)
            def _():
                getattr(copy, what)()

    def while_waiting():
        clear_edges(v1_ref)
        clear_edges(v2_ref)
        for col in range(cells // 128):
            tsc[col, time_len:, :] = jnp.zeros((8, 128), F32)
        spread[...] = jnp.zeros_like(spread)
        for guard, ref in zip(has_prev, (from_row, from_col, from_cor)):
            @pl.when(jnp.logical_not(guard))
            def _():
                ref[...] = jnp.zeros_like(ref)

    exchange(while_waiting, nx, ni * nx, cap, w_ref, tgt_ref, slot_ref, unit_ref, base_ref, d_in, m_ref, d_ref,
             whl, rank, grid_sel, meta_out, meta_in, send, got, acc, fold, basep, moves,
             send_sem, recv_sem, msend_sem, mrecv_sem)

    lane = iota((kt, 128), 1) // 16
    turned = m_ref[...].T
    for col in range(cells // 128):
        tsc[col, :time_len, :] = turned[:, col * 128:(col + 1) * 128]
    for col in range(cells // 128):
        parts = [tsc[col, pl.ds(g, kt, stride=4), :] for g in range(8)]
        for e in range(8):
            b = col * 8 + e
            v = parts[e]
            for g in range(8):
                if g != e:
                    v = jnp.where(lane == g, pltpu.roll(parts[g], ((g - e) * 16) % 128, 1), v)
            cube[b] = v
            v1_ref[b // blocks, b % blocks] = v.astype(BF16)
    sends = halo_copies(v1_ref, 0)
    run(sends, has_prev, "start")
    run(sends, has_next, "wait_recv")

    for i in range(blocks):
        first = shrink_codes(step_size * jnp.dot(patches_of(v1_ref, i, blocks), d_ref[...],
                                                 preferred_element_type=F32))
        back = lax.dot_general(first.astype(BF16), d_ref[...], (((1,), (1,)), ((), ())),
                               preferred_element_type=F32)
        for j in range(blocks):
            for sa in (0, 1):
                for sb in (0, 1):
                    g = (2 * sa + sb) * 128
                    spread[i + sa, j + sb] += back[j * kt:(j + 1) * kt, g:g + 128]
    for j in range(blocks):
        out_half[j] = fold_time(spread[blocks, j]).astype(BF16)
        out_half[blocks + j] = fold_time(spread[j, blocks]).astype(BF16)
    out_half[2 * blocks] = fold_time(spread[blocks, blocks]).astype(BF16)
    ends = [(out_half.at[pl.ds(0, blocks)], from_row), (out_half.at[pl.ds(blocks, blocks)], from_col),
            (out_half.at[2 * blocks], from_cor)]
    terms = [pltpu.make_async_remote_copy(
        src, dst, ssem.at[1, m], rsem.at[1, m],
        device_id=(mi + steps[m][0], mx + steps[m][1]), device_id_type=MESH)
        for m, (src, dst) in enumerate(ends)]
    run(terms, has_next, "start")

    def finish(i, j, more):
        b = i * blocks + j
        whole = fold_time(spread[i, j])
        for term in more:
            whole = whole + term.astype(F32)
        left = cube[b] - whole
        cube[b] = left
        v2_ref[i, j] = widen_time(left).astype(BF16)

    for i in range(1, blocks):
        for j in range(1, blocks):
            finish(i, j, [])
    run(terms, has_prev, "wait_recv")
    finish(0, 0, [from_row[0], from_col[0], from_cor[...]])
    for j in range(1, blocks):
        finish(0, j, [from_row[j]])
        finish(j, 0, [from_col[j]])
    last = halo_copies(v2_ref, 2)
    run(last, has_prev, "start")

    for col in range(cells // 128):
        parts = [cube[col * 8 + e] for e in range(8)]
        for s in range(4):
            v = parts[s]
            for e in range(8):
                if e != s:
                    v = jnp.where(lane == e, pltpu.roll(parts[e], ((e - s) * 16) % 128, 1), v)
            tsc[col, pl.ds(s, kt, stride=4), :] = v
    flat = jnp.concatenate([tsc[col, :time_len, :] for col in range(cells // 128)], axis=1).T
    for bi in range(blocks):
        for bj in range(blocks):
            for a in range(4):
                at = (bi * blocks + bj) * 16 + a * 4
                res_ref[4 * bi + a, 4 * bj:4 * bj + 4, :] = flat[at:at + 4, :]
    run(last, has_next, "wait_recv")
    run(sends, has_prev, "wait_send")
    run(terms, has_next, "wait_send")
    run(last, has_prev, "wait_send")
    exchange_end(ni * nx, send, got, meta_in, send_sem, msend_sem)


def codes_kernel(v1_ref, v2_ref, d_ref, held_ref, out_ref, res_ref):
    blocks = v1_ref.shape[0] - 1
    i = pl.program_id(0)
    first = shrink_codes(step_size * jnp.dot(patches_of(v1_ref, i, blocks), d_ref[...],
                                             preferred_element_type=F32))
    again = step_size * jnp.dot(patches_of(v2_ref, i, blocks), d_ref[...], preferred_element_type=F32)
    res_ref[...] = held_ref[...]
    out_ref[...] = shrink_codes(first + again).reshape(out_ref.shape)


def body(ni, nx, base_volume, vintage_traces, dest_device, dest_slot, vintage_id, vintage_gains, dictionary):
    side, time_len = base_volume.shape[0], base_volume.shape[2]
    n = ni * nx
    traces = vintage_traces.shape[0]
    cap = 2 * traces // n
    blocks, kt, cells = side // 4, time_len // 4, side * side
    atoms = dictionary.shape[1]
    table = vintage_id[:, None] == jnp.arange(vintage_gains.shape[0], dtype=jnp.int32)[None, :]
    gain = jnp.sum(jnp.where(table, vintage_gains[None, :], 0.0), axis=1)
    weighted = vintage_traces * gain[:, None]
    largest = jnp.max(jnp.abs(weighted), axis=1)
    unit = jnp.full((traces,), 16.0, F32)
    for power in range(3, -31, -1):
        unit = jnp.where(largest < 2.0 ** power, 2.0 ** power, unit)
    whole_steps = jnp.clip(jnp.round(weighted * (FULL / unit)[:, None]), 1.0 - FULL, FULL - 1.0)
    vmem = pl.BlockSpec(memory_space=pltpu.VMEM)
    dma = pltpu.SemaphoreType.DMA
    halo = (blocks + 1, blocks + 1, kt, 128)
    ordered, v1, v2, held = pl.pallas_call(
        functools.partial(main_kernel, ni, nx, cap),
        out_shape=(jax.ShapeDtypeStruct(dictionary.shape, BF16),
                   jax.ShapeDtypeStruct(halo, BF16), jax.ShapeDtypeStruct(halo, BF16),
                   jax.ShapeDtypeStruct(base_volume.shape, F32)),
        in_specs=[vmem] * 6, out_specs=(vmem,) * 4,
        scratch_shapes=[
            pltpu.VMEM((cells, time_len), F32),
            pltpu.VMEM((traces, 2 * time_len), BF16), pltpu.VMEM((n, traces), F32),
            pltpu.VMEM((256, traces), BF16), pltpu.VMEM((n * cap // 256, 2, 256), F32),
            pltpu.VMEM((n, 2, 256), F32), pltpu.VMEM((n, cap, time_len), WIRE),
            pltpu.VMEM((n, cap, time_len), WIRE), pltpu.VMEM((cells, time_len), F32),
            pltpu.VMEM((cells, 256), F32), pltpu.VMEM((cells, time_len), F32),
            pltpu.VMEM((256 // cap, 256, 256), BF16),
            dma, dma((n,)), dma, dma((n,)),
            pltpu.VMEM((cells // 128, time_len + 8, 128), F32), pltpu.VMEM((blocks * blocks, kt, 128), F32),
            pltpu.VMEM(halo, F32), pltpu.VMEM((2 * blocks + 1, kt, 128), BF16),
            pltpu.VMEM((blocks, kt, 128), BF16), pltpu.VMEM((blocks, kt, 128), BF16),
            pltpu.VMEM((kt, 128), BF16), dma((3, 3)), dma((3, 3))],
        compiler_params=pltpu.CompilerParams(collective_id=0, has_side_effects=True,
                                             vmem_limit_bytes=40 << 20),
        name="merge_and_iterate",
    )(whole_steps, dest_device.reshape(1, traces), dest_slot.reshape(1, traces), unit.reshape(1, traces),
      base_volume, dictionary)
    slab = pl.BlockSpec((4, side, time_len), lambda i: (i, 0, 0))
    whole = lambda *shape: pl.BlockSpec(shape, lambda i: (0,) * len(shape))
    codes, residual = pl.pallas_call(
        codes_kernel,
        grid=(blocks,),
        out_shape=(jax.ShapeDtypeStruct((blocks, blocks, kt, atoms), F32),
                   jax.ShapeDtypeStruct(base_volume.shape, F32)),
        in_specs=[whole(*halo), whole(*halo), whole(512, atoms), slab],
        out_specs=(pl.BlockSpec((1, blocks, kt, atoms), lambda i: (i, 0, 0, 0)), slab),
        compiler_params=pltpu.CompilerParams(vmem_limit_bytes=40 << 20),
        name="codes",
    )(v1, v2, ordered, held)
    return codes, residual


def solution(mesh):
    in_specs = (
        P("inline", "xline", None),
        P(("inline", "xline"), None),
        P(("inline", "xline"), None),
        P(("inline", "xline")),
        P(("inline", "xline")),
        P(),
        P(),
    )
    out_specs = (P("inline", "xline", None, None), P("inline", "xline", None))
    return jax.shard_map(functools.partial(body, mesh.shape["inline"], mesh.shape["xline"]),
                         mesh=mesh, in_specs=in_specs, out_specs=out_specs, check_vma=False)
```

```python
import functools
import jax
import jax.numpy as jnp
from jax import lax
from jax.experimental import pallas as pl
from jax.experimental.pallas import tpu as pltpu
from jax.sharding import PartitionSpec as P

step_size = 0.25
threshold = 0.02
WIRE = jnp.int16
FULL = 32768.0
MESH = pl.DeviceIdType.MESH
F32, BF16 = jnp.float32, jnp.bfloat16


def shrink_codes(values):
    return values - jnp.clip(values, -threshold, threshold)


def iota(shape, dim):
    return lax.broadcasted_iota(jnp.int32, shape, dim)


def split_half(x):
    hi = x.astype(BF16)
    return hi, (x - hi.astype(F32)).astype(BF16)


def exchange(while_waiting, nx, n, cap, w_ref, tgt_ref, slot_ref, unit_ref, base_ref, d_in, out_ref, d_ref, whl, rank, grid_sel,
                    meta_out, meta_in, send, got, acc, fold, basep, moves,
                    send_sem, recv_sem, msend_sem, mrecv_sem):
    me = lax.axis_index("inline") * nx + lax.axis_index("xline")
    side, time_len = base_ref.shape[0], base_ref.shape[2]
    blocks = side // 4
    bins = side * side
    traces = w_ref.shape[0]
    q = 256 // cap
    chunks = n // q

    def where_is(p):
        return (p // nx, p % nx)

    barrier = pltpu.get_barrier_semaphore()

    @pl.loop(1, n)
    def _(off):
        pl.semaphore_signal(barrier, inc=1, device_id=where_is((me + off) % n), device_id_type=MESH)

    hi, lo = split_half(w_ref[...])
    whl[:, :time_len] = hi
    whl[:, time_len:] = lo
    tri = (iota((128, 128), 0) <= iota((128, 128), 1)).astype(F32).astype(BF16)
    base_count = jnp.zeros((n, 1), F32)
    for b in range(traces // 128):
        mine = tgt_ref[:, b * 128:(b + 1) * 128] == iota((n, 128), 0)
        one = jnp.where(mine, 1.0, 0.0)
        cum = jnp.dot(one.astype(BF16), tri, preferred_element_type=F32) + base_count
        rank[:, b * 128:(b + 1) * 128] = jnp.where(mine, cum - 1.0, -1.0)
        base_count = base_count + jnp.sum(one, axis=1, keepdims=True)
    slot = slot_ref[...]
    r, c = slot // side, slot % side
    binned = ((r // 4) * blocks + c // 4) * 16 + (r % 4) * 4 + c % 4
    first_row = iota((16, traces), 0) == 0
    about = jnp.where(first_row, (binned + 1).astype(F32), unit_ref[...]).astype(BF16)
    my_q = me % q
    lane_from, lane_to = iota((256, 256), 0), iota((256, 256), 1)
    for i in range(q):
        move = (lane_from - my_q * cap == lane_to - i * cap) & (lane_to // cap == i)
        moves[i] = jnp.where(move, 1.0, 0.0).astype(BF16)
    for bi in range(blocks):
        for bj in range(blocks):
            for a in range(4):
                at = (bi * blocks + bj) * 16 + a * 4
                basep[at:at + 4, :] = base_ref[4 * bi + a, 4 * bj:4 * bj + 4, :]
    acc[...] = jnp.zeros_like(acc)
    fold[...] = jnp.zeros_like(fold)

    @pl.loop(0, chunks)
    def _(step):
        off = (2 * step + 1) % chunks + (2 * step + 1) // chunks
        ch = (me // q + off) % chunks
        want = iota((cap, traces), 0).astype(F32)
        for i in range(q):
            row = rank[pl.ds(ch * q + i, 1), :]
            grid_sel[i * cap:(i + 1) * cap, :] = jnp.where(row == want, 1.0, 0.0).astype(BF16)
        sel = grid_sel[...]
        picked = jnp.dot(sel, whl[...], preferred_element_type=F32)
        packed = (picked[:, :time_len] + picked[:, time_len:]).astype(jnp.int32).astype(WIRE)
        names = lax.dot_general(about, sel, (((1,), (1,)), ((), ())), preferred_element_type=F32)
        meta_out[ch] = names[0:2, :]
        for i in range(q):
            send[ch * q + i] = packed[i * cap:(i + 1) * cap, :]

        @pl.when(step == 0)
        def _():
            pl.semaphore_wait(barrier, n - 1)

        for i in range(q):
            p = ch * q + i

            @pl.when(p != me)
            def _():
                pltpu.make_async_remote_copy(
                    meta_out.at[ch], meta_in.at[me], msend_sem, mrecv_sem.at[me],
                    device_id=where_is(p), device_id_type=MESH).start()
                pltpu.make_async_remote_copy(
                    send.at[p], got.at[me], send_sem, recv_sem.at[me],
                    device_id=where_is(p), device_id_type=MESH).start()

            @pl.when(p == me)
            def _():
                meta_in[me] = meta_out[ch]
                got[me] = send[p]

    rows_of, cols_of = iota((512, 512), 0), iota((512, 512), 1)
    wanted = ((rows_of // 256) * 256 + (rows_of % 16) // 4 * 64 + (rows_of // 128 % 2) * 32
              + (rows_of % 4) * 8 + rows_of // 16 % 8)
    d_ref[...] = jnp.dot(jnp.where(wanted == cols_of, 1.0, 0.0).astype(BF16), d_in[...],
                         preferred_element_type=F32).astype(BF16)
    while_waiting()

    @pl.loop(0, chunks)
    def _(step):
        off = (2 * step + 1) % chunks + (2 * step + 1) // chunks
        ch = (me // q + 2 * chunks - off) % chunks
        names = jnp.zeros((16, 256), F32)
        for i in range(q):
            src = ch * q + i

            @pl.when(src != me)
            def _():
                pltpu.make_async_remote_copy(
                    meta_out.at[0], meta_in.at[src], msend_sem, mrecv_sem.at[src],
                    device_id=where_is(src), device_id_type=MESH).wait_recv()
                pltpu.make_async_remote_copy(
                    send.at[src], got.at[src], send_sem, recv_sem.at[src],
                    device_id=where_is(src), device_id_type=MESH).wait_recv()

            both = meta_in[src]
            row = jnp.where(iota((16, 256), 0) == 0, both[0:1, :], both[1:2, :]).astype(BF16)
            names = names + jnp.dot(row, moves[i], preferred_element_type=F32)
        hit = jnp.where(names[0:1, :] == (iota((bins, 256), 0) + 1).astype(F32), 1.0, 0.0)
        rows = got[pl.ds(ch * q, q)].astype(jnp.int32).astype(F32).reshape(256, time_len)
        hi, lo = split_half(rows)
        half = (hit * names[1:2, :]).astype(BF16)
        acc[...] += jnp.dot(half, hi, preferred_element_type=F32) + jnp.dot(half, lo, preferred_element_type=F32)
        fold[...] += hit

    count = jnp.sum(fold[...], axis=1, keepdims=True)
    out_ref[...] = (basep[...] + acc[...] * (1.0 / FULL)) / (1.0 + count)


def exchange_end(n, send, got, meta_in, send_sem, msend_sem):
    all_data = send.at[pl.ds(0, n - 1)]
    pltpu.make_async_copy(all_data, got.at[pl.ds(0, n - 1)], send_sem).wait()
    pltpu.make_async_copy(meta_in.at[pl.ds(0, n - 1)], meta_in.at[pl.ds(0, n - 1)], msend_sem).wait()


def patches_of(v_ref, i, blocks):
    rows = []
    for j in range(blocks):
        rows.append(jnp.concatenate(
            [v_ref[i + sa, j + sb] for sa in (0, 1) for sb in (0, 1)], axis=1))
    return jnp.concatenate(rows, axis=0)


def fold_time(x):
    rolled = pltpu.roll(x, 64, 1)
    rolled = pltpu.roll(rolled, 1, 0)
    return x + jnp.where(iota(x.shape, 0) == 0, 0.0, rolled)


def widen_time(x):
    ahead = pltpu.roll(pltpu.roll(x, 64, 1), x.shape[0] - 1, 0)
    ahead = jnp.where(iota(x.shape, 0) == x.shape[0] - 1, 0.0, ahead)
    return jnp.where(iota(x.shape, 1) < 64, x, ahead)


def main_kernel(ni, nx, cap, w_ref, tgt_ref, slot_ref, unit_ref, base_ref, d_in,
                d_ref, v1_ref, v2_ref, res_ref,
                m_ref, whl, rank, grid_sel, meta_out, meta_in, send, got, acc, fold, basep, moves,
                send_sem, recv_sem, msend_sem, mrecv_sem,
                tsc, cube, spread, out_half, from_row, from_col, from_cor, ssem, rsem):
    mi, mx = lax.axis_index("inline"), lax.axis_index("xline")
    blocks = v1_ref.shape[0] - 1
    kt = v1_ref.shape[2]
    cells, time_len = m_ref.shape
    has_prev = [mi > 0, mx > 0, (mi > 0) & (mx > 0)]
    has_next = [mi < ni - 1, mx < nx - 1, (mi < ni - 1) & (mx < nx - 1)]
    steps = [(1, 0), (0, 1), (1, 1)]

    def halo_copies(v_ref, slot):
        pairs = [(v_ref.at[0, pl.ds(0, blocks)], v_ref.at[blocks, pl.ds(0, blocks)]),
                 (v_ref.at[pl.ds(0, blocks), 0], v_ref.at[pl.ds(0, blocks), blocks]),
                 (v_ref.at[0, 0], v_ref.at[blocks, blocks])]
        return [pltpu.make_async_remote_copy(
            src, dst, ssem.at[slot, m], rsem.at[slot, m],
            device_id=(mi - steps[m][0], mx - steps[m][1]), device_id_type=MESH)
            for m, (src, dst) in enumerate(pairs)]

    def clear_edges(v_ref):
        blank = jnp.zeros((kt, 128), BF16)

        @pl.when(mi == ni - 1)
        def _():
            for j in range(blocks + 1):
                v_ref[blocks, j] = blank

        @pl.when(mx == nx - 1)
        def _():
            for i in range(blocks + 1):
                v_ref[i, blocks] = blank

    def run(copies, guards, what):
        for copy, guard in zip(copies, guards):
            @pl.when(guard)
            def _():
                getattr(copy, what)()

    def while_waiting():
        clear_edges(v1_ref)
        clear_edges(v2_ref)
        for col in range(cells // 128):
            tsc[col, time_len:, :] = jnp.zeros((8, 128), F32)
        spread[...] = jnp.zeros_like(spread)
        for guard, ref in zip(has_prev, (from_row, from_col, from_cor)):
            @pl.when(jnp.logical_not(guard))
            def _():
                ref[...] = jnp.zeros_like(ref)

    exchange(while_waiting, nx, ni * nx, cap, w_ref, tgt_ref, slot_ref, unit_ref, base_ref, d_in, m_ref, d_ref,
             whl, rank, grid_sel, meta_out, meta_in, send, got, acc, fold, basep, moves,
             send_sem, recv_sem, msend_sem, mrecv_sem)

    lane = iota((kt, 128), 1) // 16
    turned = m_ref[...].T
    for col in range(cells // 128):
        tsc[col, :time_len, :] = turned[:, col * 128:(col + 1) * 128]
    for col in range(cells // 128):
        parts = [tsc[col, pl.ds(g, kt, stride=4), :] for g in range(8)]
        for e in range(8):
            b = col * 8 + e
            v = parts[e]
            for g in range(8):
                if g != e:
                    v = jnp.where(lane == g, pltpu.roll(parts[g], ((g - e) * 16) % 128, 1), v)
            cube[b] = v
            v1_ref[b // blocks, b % blocks] = v.astype(BF16)
    sends = halo_copies(v1_ref, 0)
    run(sends, has_prev, "start")
    run(sends, has_next, "wait_recv")

    for i in range(blocks):
        first = shrink_codes(step_size * jnp.dot(patches_of(v1_ref, i, blocks), d_ref[...],
                                                 preferred_element_type=F32))
        back = lax.dot_general(first.astype(BF16), d_ref[...], (((1,), (1,)), ((), ())),
                               preferred_element_type=F32)
        for j in range(blocks):
            for sa in (0, 1):
                for sb in (0, 1):
                    g = (2 * sa + sb) * 128
                    spread[i + sa, j + sb] += back[j * kt:(j + 1) * kt, g:g + 128]
    for j in range(blocks):
        out_half[j] = fold_time(spread[blocks, j]).astype(BF16)
        out_half[blocks + j] = fold_time(spread[j, blocks]).astype(BF16)
    out_half[2 * blocks] = fold_time(spread[blocks, blocks]).astype(BF16)
    ends = [(out_half.at[pl.ds(0, blocks)], from_row), (out_half.at[pl.ds(blocks, blocks)], from_col),
            (out_half.at[2 * blocks], from_cor)]
    terms = [pltpu.make_async_remote_copy(
        src, dst, ssem.at[1, m], rsem.at[1, m],
        device_id=(mi + steps[m][0], mx + steps[m][1]), device_id_type=MESH)
        for m, (src, dst) in enumerate(ends)]
    run(terms, has_next, "start")

    def finish(i, j, more):
        b = i * blocks + j
        whole = fold_time(spread[i, j])
        for term in more:
            whole = whole + term.astype(F32)
        left = cube[b] - whole
        cube[b] = left
        v2_ref[i, j] = widen_time(left).astype(BF16)

    for i in range(1, blocks):
        for j in range(1, blocks):
            finish(i, j, [])
    run(terms, has_prev, "wait_recv")
    finish(0, 0, [from_row[0], from_col[0], from_cor[...]])
    for j in range(1, blocks):
        finish(0, j, [from_row[j]])
        finish(j, 0, [from_col[j]])
    last = halo_copies(v2_ref, 2)
    run(last, has_prev, "start")

    for col in range(cells // 128):
        parts = [cube[col * 8 + e] for e in range(8)]
        for s in range(4):
            v = parts[s]
            for e in range(8):
                if e != s:
                    v = jnp.where(lane == e, pltpu.roll(parts[e], ((e - s) * 16) % 128, 1), v)
            tsc[col, pl.ds(s, kt, stride=4), :] = v
    flat = jnp.concatenate([tsc[col, :time_len, :] for col in range(cells // 128)], axis=1).T
    for bi in range(blocks):
        for bj in range(blocks):
            for a in range(4):
                at = (bi * blocks + bj) * 16 + a * 4
                res_ref[4 * bi + a, 4 * bj:4 * bj + 4, :] = flat[at:at + 4, :]
    run(last, has_next, "wait_recv")
    run(sends, has_prev, "wait_send")
    run(terms, has_next, "wait_send")
    run(last, has_prev, "wait_send")
    exchange_end(ni * nx, send, got, meta_in, send_sem, msend_sem)


def codes_kernel(v1_ref, v2_ref, d_ref, held_ref, out_ref, res_ref):
    blocks = v1_ref.shape[0] - 1
    i = pl.program_id(0)
    first = shrink_codes(step_size * jnp.dot(patches_of(v1_ref, i, blocks), d_ref[...],
                                             preferred_element_type=F32))
    again = step_size * jnp.dot(patches_of(v2_ref, i, blocks), d_ref[...], preferred_element_type=F32)
    res_ref[...] = held_ref[...]
    out_ref[...] = shrink_codes(first + again).reshape(out_ref.shape)


def body(ni, nx, base_volume, vintage_traces, dest_device, dest_slot, vintage_id, vintage_gains, dictionary):
    side, time_len = base_volume.shape[0], base_volume.shape[2]
    n = ni * nx
    traces = vintage_traces.shape[0]
    cap = 2 * traces // n
    blocks, kt, cells = side // 4, time_len // 4, side * side
    atoms = dictionary.shape[1]
    table = vintage_id[:, None] == jnp.arange(vintage_gains.shape[0], dtype=jnp.int32)[None, :]
    gain = jnp.sum(jnp.where(table, vintage_gains[None, :], 0.0), axis=1)
    weighted = vintage_traces * gain[:, None]
    largest = jnp.max(jnp.abs(weighted), axis=1)
    unit = jnp.full((traces,), 16.0, F32)
    for power in range(3, -31, -1):
        unit = jnp.where(largest < 2.0 ** power, 2.0 ** power, unit)
    whole_steps = jnp.clip(jnp.round(weighted * (FULL / unit)[:, None]), 1.0 - FULL, FULL - 1.0)
    vmem = pl.BlockSpec(memory_space=pltpu.VMEM)
    dma = pltpu.SemaphoreType.DMA
    halo = (blocks + 1, blocks + 1, kt, 128)
    ordered, v1, v2, held = pl.pallas_call(
        functools.partial(main_kernel, ni, nx, cap),
        out_shape=(jax.ShapeDtypeStruct(dictionary.shape, BF16),
                   jax.ShapeDtypeStruct(halo, BF16), jax.ShapeDtypeStruct(halo, BF16),
                   jax.ShapeDtypeStruct(base_volume.shape, F32)),
        in_specs=[vmem] * 6, out_specs=(vmem,) * 4,
        scratch_shapes=[
            pltpu.VMEM((cells, time_len), F32),
            pltpu.VMEM((traces, 2 * time_len), BF16), pltpu.VMEM((n, traces), F32),
            pltpu.VMEM((256, traces), BF16), pltpu.VMEM((n * cap // 256, 2, 256), F32),
            pltpu.VMEM((n, 2, 256), F32), pltpu.VMEM((n, cap, time_len), WIRE),
            pltpu.VMEM((n, cap, time_len), WIRE), pltpu.VMEM((cells, time_len), F32),
            pltpu.VMEM((cells, 256), F32), pltpu.VMEM((cells, time_len), F32),
            pltpu.VMEM((256 // cap, 256, 256), BF16),
            dma, dma((n,)), dma, dma((n,)),
            pltpu.VMEM((cells // 128, time_len + 8, 128), F32), pltpu.VMEM((blocks * blocks, kt, 128), F32),
            pltpu.VMEM(halo, F32), pltpu.VMEM((2 * blocks + 1, kt, 128), BF16),
            pltpu.VMEM((blocks, kt, 128), BF16), pltpu.VMEM((blocks, kt, 128), BF16),
            pltpu.VMEM((kt, 128), BF16), dma((3, 3)), dma((3, 3))],
        compiler_params=pltpu.CompilerParams(collective_id=0, has_side_effects=True,
                                             vmem_limit_bytes=40 << 20),
        name="merge_and_iterate",
    )(whole_steps, dest_device.reshape(1, traces), dest_slot.reshape(1, traces), unit.reshape(1, traces),
      base_volume, dictionary)
    slab = pl.BlockSpec((4, side, time_len), lambda i: (i, 0, 0))
    whole = lambda *shape: pl.BlockSpec(shape, lambda i: (0,) * len(shape))
    codes, residual = pl.pallas_call(
        codes_kernel,
        grid=(blocks,),
        out_shape=(jax.ShapeDtypeStruct((blocks, blocks, kt, atoms), F32),
                   jax.ShapeDtypeStruct(base_volume.shape, F32)),
        in_specs=[whole(*halo), whole(*halo), whole(512, atoms), slab],
        out_specs=(pl.BlockSpec((1, blocks, kt, atoms), lambda i: (i, 0, 0, 0)), slab),
        compiler_params=pltpu.CompilerParams(vmem_limit_bytes=40 << 20),
        name="codes",
    )(v1, v2, ordered, held)
    return codes, residual


def solution(mesh):
    in_specs = (
        P("inline", "xline", None),
        P(("inline", "xline"), None),
        P(("inline", "xline"), None),
        P(("inline", "xline")),
        P(("inline", "xline")),
        P(),
        P(),
    )
    out_specs = (P("inline", "xline", None, None), P("inline", "xline", None))
    return jax.shard_map(functools.partial(body, mesh.shape["inline"], mesh.shape["xline"]),
                         mesh=mesh, in_specs=in_specs, out_specs=out_specs, check_vma=False)
```
